32 devices in a mesh: band: 4 (over y, x), dev: 8 (over z, core).
Axes of the slice: x: 2, y: 2, z: 4, core: 2. Of those that a mesh axis runs over, the one named last changes fastest.
Arguments:
- waves: bfloat16 [4, 512, 256], P('band', 'dev'), may hold values from -6 to 6
- tile_list: int32 [4, 32, 3], P('band', 'dev'), may hold values from 0 to 7, as said below
- tile_count: int32 [4, 8], P('band', 'dev'), may hold values from 1 to 4, as said below
- pair_mask: int32 [4, 32, 4096], P('band', 'dev'), may hold values 0 or 1
Outputs:
- peaks: float32 [4, 32, 4096], P('band', 'dev')
The draws below stay inside these ranges and needn't reach their ends.
Inputs may be any that keep to these rules, and one draw needn't show every extreme that they name: `tile_list`: column 0 is a block of 64 events in the device's own band, column 1 is one plus the offset (-1, 0 or 1) of the other band, which always lies within the bands, column 2 is a block of 64 events in the other band. `tile_count`: slots at or beyond the count hold no tile; some device uses all 4 slots.
All inputs are finite; a program needn't handle non-finite values. No bound on the sum of `pair_mask` on one device may be relied on, other than what follows from the above.
Results may differ from the reference program's by a relative error of at most 0.0025.
Values may be sent and summed in bfloat16 or wider, within the bound.
No kernel may reach another device: no remote copies, remote signals or barrier semaphores. Data moves between devices by JAX's collectives and lax.ppermute only.
A program may use at most 64 MiB of HBM per device.

```python
import math
import jax
import jax.numpy as jnp
from jax import lax

SAMPLES = 256
FFT_LEN = 512
TILE = 64
TILES_DEV = 4
BANDS = 4
EV_BAND = 512
TILES_ALL = 32
N_DEV = 8


def draw_tile_list(key, part):
    key_rows = jax.random.fold_in(key, 11)
    key_off = jax.random.fold_in(key, 12)
    key_cols = jax.random.fold_in(key, 13)
    shape = (BANDS, TILES_ALL, 1)
    rows = jax.random.randint(key_rows, shape, 0, EV_BAND // TILE, dtype=jnp.int32)
    cols = jax.random.randint(key_cols, shape, 0, EV_BAND // TILE, dtype=jnp.int32)
    offset = jax.random.randint(key_off, shape, 0, 3, dtype=jnp.int32)
    band_idx = lax.broadcasted_iota(jnp.int32, shape, 0)
    offset = jnp.where(band_idx == 0, jnp.maximum(offset, 1), offset)
    offset = jnp.where(band_idx == BANDS - 1, jnp.minimum(offset, 1), offset)
    return jnp.concatenate([rows, offset, cols], axis=-1).astype(jnp.int32)


def draw_tile_count(key, part):
    key_heavy = jax.random.fold_in(key, 21)
    key_light = jax.random.fold_in(key, 22)
    key_place = jax.random.fold_in(key, 23)
    shape = (BANDS, N_DEV)
    heavy = jax.random.randint(key_heavy, shape, 0, 4, dtype=jnp.int32) == 0
    light = jax.random.randint(key_light, shape, 1, min(3, TILES_DEV + 1), dtype=jnp.int32)
    counts = jnp.where(heavy, TILES_DEV, light).reshape(BANDS * N_DEV)
    place = jax.random.randint(key_place, (), 0, BANDS * N_DEV, dtype=jnp.int32)
    flat_idx = jnp.arange(BANDS * N_DEV, dtype=jnp.int32)
    counts = jnp.where(flat_idx == place, TILES_DEV, counts)
    return counts.reshape(BANDS, N_DEV).astype(jnp.int32)


def with_ends(drawn, stream_key, low, high):
    spot = [jax.random.randint(jax.random.fold_in(stream_key, axis), (), 0, length) for axis, length in enumerate(drawn.shape)]
    widest = drawn.shape.index(max(drawn.shape))
    next_to = spot[:widest] + [(spot[widest] + 1) % drawn.shape[widest]] + spot[widest + 1:]
    return drawn.at[tuple(spot)].set(low).at[tuple(next_to)].set(high)


def block_scale(rng, shape, pieces, least, largest):
    level = 1.0
    for axis_at, parts in pieces:
        steps = jax.random.uniform(jax.random.fold_in(jax.random.fold_in(rng, 6), axis_at), (parts,), jnp.float32, least / len(pieces), largest / len(pieces))
        level = level * jnp.repeat(jnp.exp(steps), shape[axis_at] // parts).reshape((-1,) + (1,) * (len(shape) - 1 - axis_at))
    return level


def centred(key, dims, deviation, most, pieces=(), held_as=jnp.bfloat16):
    entries = deviation * jax.random.normal(key, dims, jnp.float32)
    if pieces:
        entries = entries * block_scale(key, dims, pieces, -0.22, 0.18)
    return jnp.clip(entries, -most, most).astype(held_as)


def setup_inputs(seed: int = 0) -> dict:
    seeds = jax.random.split(jax.random.key(seed), 5)
    return {
        "waves": centred(seeds[0], (BANDS, EV_BAND, SAMPLES), 1.0, 6.0, ((0, 4), (1, 8))),
        "tile_list": draw_tile_list(jax.random.fold_in(seeds[4], 71), 0),
        "tile_count": draw_tile_count(jax.random.fold_in(seeds[4], 71), 0),
        "pair_mask": with_ends((jax.random.randint(seeds[3], (BANDS, TILES_ALL, TILE * TILE), 0, 2) < 1).astype(jnp.int32), jax.random.fold_in(seeds[3], 1), 0, 1),
    }


def forward_table():
    rows = jnp.arange(SAMPLES, dtype=jnp.int32)[:, None]
    cols = jnp.arange(SAMPLES, dtype=jnp.int32)[None, :]
    angle = 2.0 * math.pi / FFT_LEN * (rows * cols % FFT_LEN).astype(jnp.float32)
    return jnp.concatenate([jnp.cos(angle), -jnp.sin(angle)], axis=1).astype(jnp.bfloat16)

def inverse_table():
    rows = jnp.arange(SAMPLES, dtype=jnp.int32)[:, None]
    cols = jnp.arange(FFT_LEN, dtype=jnp.int32)[None, :]
    angle = 2.0 * math.pi / FFT_LEN * (rows * cols % FFT_LEN).astype(jnp.float32)
    weight = jnp.where(rows == 0, 1.0, 2.0).astype(jnp.float32) / FFT_LEN
    return jnp.concatenate([weight * jnp.cos(angle), -weight * jnp.sin(angle)], axis=0).astype(jnp.bfloat16)

def make_spectra(wave_rows):
    values = wave_rows.astype(jnp.float32)
    energy = lax.optimization_barrier(jnp.sum(values * values, axis=-1, keepdims=True)) + 1e-06
    unit = (values / jnp.sqrt(energy)).astype(jnp.bfloat16)
    return jnp.dot(unit, forward_table(), preferred_element_type=jnp.float32).astype(jnp.bfloat16)

def tile_peaks(own, other, mask_row, inverse):
    half = own.shape[1] // 2
    own_re = own[:, :half].astype(jnp.float32)
    own_im = own[:, half:].astype(jnp.float32)
    oth_re = other[:, :half].astype(jnp.float32)
    oth_im = other[:, half:].astype(jnp.float32)
    real_part = own_re[:, None, :] * oth_re[None, :, :] + own_im[:, None, :] * oth_im[None, :, :]
    imag_part = own_im[:, None, :] * oth_re[None, :, :] - own_re[:, None, :] * oth_im[None, :, :]
    count = own.shape[0] * other.shape[0]
    cross = jnp.concatenate([real_part, imag_part], axis=-1).reshape(count, 2 * half).astype(jnp.bfloat16)
    corr = jnp.dot(cross, inverse, preferred_element_type=jnp.float32)
    return lax.optimization_barrier(jnp.max(corr, axis=-1)) * mask_row.astype(jnp.float32)

def reference(waves, tile_list, tile_count, pair_mask):
    spectra = make_spectra(waves.reshape(BANDS * EV_BAND, SAMPLES))
    inverse = inverse_table()
    flat_list = tile_list.reshape(BANDS * TILES_ALL, 3)
    flat_mask = pair_mask.reshape(BANDS * TILES_ALL, TILE * TILE)
    counts = tile_count.reshape(BANDS * N_DEV)
    slots = jnp.arange(BANDS * TILES_ALL, dtype=jnp.int32)

    def one_tile(item):
        entry, mask_row, slot = item
        band_idx = slot // TILES_ALL
        used = slot % TILES_DEV < counts[slot // TILES_DEV]
        own_start = (band_idx * EV_BAND + entry[0] * TILE).astype(jnp.int32)
        other_start = ((band_idx + entry[1] - 1) * EV_BAND + entry[2] * TILE).astype(jnp.int32)

        def compute(unused):
            own = lax.dynamic_slice_in_dim(spectra, own_start, TILE, 0)
            other = lax.dynamic_slice_in_dim(spectra, other_start, TILE, 0)
            return tile_peaks(own, other, mask_row, inverse)

        def empty(unused):
            return jnp.zeros((TILE * TILE,), jnp.float32)
        return lax.cond(used, compute, empty, 0)
    result = lax.map(one_tile, (flat_list, flat_mask, slots))
    return result.reshape(BANDS, TILES_ALL, TILE * TILE)
```

```python
import functools

import jax
import jax.numpy as jnp
from jax import lax
from jax.experimental import pallas as pl
from jax.experimental.pallas import tpu as pltpu
from jax.sharding import PartitionSpec as P

TILE = 64
LANES = 128
SHIFTS = 32
DEPTH = 2
SLOTS = 4


def normalized(rows):
    values = rows.astype(jnp.float32)
    energy = jnp.sum(values * values, axis=-1, keepdims=True) + 1e-06
    return (values / jnp.sqrt(energy)).astype(jnp.bfloat16).astype(jnp.float32)


def tile_peaks(own, other, acc_cyc, acc_neg):
    samples = own.shape[1]
    unit = normalized(own)
    half_unit = normalized(other) * 0.5
    lane = lax.broadcasted_iota(jnp.int32, (TILE, LANES), 1)
    wide = lax.broadcasted_iota(jnp.int32, (TILE, samples), 1)
    cyc, neg = [], []
    for r in range(samples // TILE):
        shifted = pltpu.roll(half_unit, SHIFTS * r, 1) if r else half_unit
        cyc.append(shifted.astype(jnp.bfloat16))
        neg.append(jnp.where(wide < SHIFTS * r, -shifted, shifted).astype(jnp.bfloat16))
    pltpu.matmul_push_rhs(jnp.concatenate(cyc, axis=0), 0, 0, transpose=True)
    pltpu.matmul_push_rhs(jnp.concatenate(neg, axis=0), 0, 1, transpose=True)
    sign = jnp.where(wide % 2 == 0, 1.0, -1.0)
    own_alt = jnp.sum(unit * sign, axis=-1, keepdims=True) * (1.0 / samples)
    pltpu.matmul_acc_lhs(acc_cyc[0], sign.astype(jnp.bfloat16), load_staged_rhs=0)
    pltpu.matmul_acc_lhs(acc_neg[0], sign.astype(jnp.bfloat16), load_staged_rhs=0)
    other_alt = pltpu.matmul_pop(acc_cyc[0])[0:1]
    pltpu.matmul_pop(acc_neg[0])
    low, high = unit[:, :LANES], unit[:, LANES:]
    count = len(acc_cyc) // 2

    def push(s):
        at = 2 * (s % count)
        first = pltpu.roll(low, LANES - s, 1) if s else low
        second = pltpu.roll(high, LANES - s, 1) if s else high
        inside = lane < LANES - s
        a = jnp.where(inside, first, second).astype(jnp.bfloat16)
        b = jnp.where(inside, second, first).astype(jnp.bfloat16)
        c = jnp.where(inside, second, -first).astype(jnp.bfloat16)
        pltpu.matmul_acc_lhs(acc_cyc[at], jnp.concatenate([a, b], axis=1))
        pltpu.matmul_acc_lhs(acc_neg[at], jnp.concatenate([a, c], axis=1))
        pltpu.matmul_acc_lhs(acc_cyc[at + 1], jnp.concatenate([b, a], axis=1))
        pltpu.matmul_acc_lhs(acc_neg[at + 1], jnp.concatenate([c, -a], axis=1))

    best = [jnp.full((TILE, samples), -jnp.inf, jnp.float32)] * 2
    for s in range(DEPTH):
        push(s)
    for s in range(SHIFTS):
        if s + DEPTH < SHIFTS:
            push(s + DEPTH)
        at = 2 * (s % count)
        for t in range(2):
            pair = pltpu.matmul_pop(acc_cyc[at + t]) + jnp.abs(pltpu.matmul_pop(acc_neg[at + t]))
            best[s % 2] = jnp.maximum(best[s % 2], pair)
    nyquist = own_alt * other_alt
    peak = jnp.maximum(best[0] - nyquist, best[1] + nyquist)
    peak = jnp.maximum(peak[:, :LANES], peak[:, LANES:])
    return jnp.maximum(peak, pltpu.roll(peak, TILE, 1))


def tiles_kernel(list_ref, count_ref, mask_ref, *refs):
    pieces, (out_ref, blocks, sems, peaks) = refs[:6], refs[6:]
    slots = out_ref.shape[0]
    used = count_ref[0, 0]
    band = lax.axis_index("band")
    dev = lax.axis_index("dev")

    def fetch(slot, which, block, offset):
        swapped = (block + dev) % 2
        place = (block // 2) ^ (dev // 2)
        odd = (band + offset // 2) % 2
        kind = jnp.where(offset == 1, 0, jnp.where(odd == 1, 1, 2))
        for k in range(3):
            for c in range(2):

                @pl.when((kind == k) & (swapped == c))
                def _():
                    pltpu.make_async_copy(
                        pieces[k + 3 * c].at[place], blocks.at[slot, which], sems.at[slot, which]
                    ).start()

    def fetch_slot(slot, carry):
        fetch(slot, 0, list_ref[slot, 0], jnp.int32(1))
        fetch(slot, 1, list_ref[slot, 2], list_ref[slot, 1])
        return carry

    lax.fori_loop(0, used, fetch_slot, 0)
    peaks[...] = jnp.zeros_like(peaks)

    def compute(*accs):
        def one_tile(slot, carry):
            for which in range(2):
                pltpu.make_async_copy(
                    pieces[0].at[0], blocks.at[slot, which], sems.at[slot, which]
                ).wait()
            peaks[pl.ds(pl.multiple_of(slot * TILE, TILE), TILE), :] = tile_peaks(
                blocks[slot, 0], blocks[slot, 1], accs[: len(accs) // 2], accs[len(accs) // 2 :]
            )
            return carry

        lax.fori_loop(0, used, one_tile, 0)

    samples = blocks.shape[3]
    pl.run_scoped(
        compute,
        *[pltpu.ACC(unit)((TILE, samples), jnp.float32) for unit in range(2) for _ in range(2 * SLOTS)],
    )
    lane = lax.broadcasted_iota(jnp.int32, (slots, LANES), 1)
    for p in range(TILE // 2):
        even = peaks[pl.ds(2 * p, slots, stride=TILE), :]
        odd = peaks[pl.ds(2 * p + 1, slots, stride=TILE), :]
        at = pl.ds(p * LANES, LANES)
        out_ref[:, at] = jnp.where(lane < TILE, even, odd) * mask_ref[:, at].astype(jnp.float32)


def tiles(tile_list, tile_count, pair_mask, pieces):
    slots = tile_list.shape[0]
    samples = pieces[0].shape[2]
    smem = pl.BlockSpec(memory_space=pltpu.SMEM)
    vmem = pl.BlockSpec(memory_space=pltpu.VMEM)
    return pl.pallas_call(
        tiles_kernel,
        out_shape=jax.ShapeDtypeStruct(pair_mask.shape, jnp.float32),
        in_specs=[smem, smem, vmem] + [pl.BlockSpec(memory_space=pltpu.HBM)] * 6,
        out_specs=vmem,
        scratch_shapes=[
            pltpu.VMEM((slots, 2, TILE, samples), jnp.bfloat16),
            pltpu.SemaphoreType.DMA((slots, 2)),
            pltpu.VMEM((slots * TILE, LANES), jnp.float32),
        ],
        compiler_params=pltpu.CompilerParams(vmem_limit_bytes=16 * 1024 * 1024),
        name="tiles",
    )(tile_list, tile_count, pair_mask, *pieces)


def matched(value, first):
    count = lax.axis_size("band")
    pairs = []
    for i in range(first, count - 1, 2):
        pairs += [(i, i + 1), (i + 1, i)]
    return lax.ppermute(value, "band", pairs)


def flipped(value, mask):
    return lax.ppermute(value, "dev", [(i, i ^ mask) for i in range(lax.axis_size("dev"))])


def body(waves, tile_list, tile_count, pair_mask):
    columns = [waves] + [flipped(waves, 2 * k) for k in range(1, lax.axis_size("dev") // 2)]
    column = jnp.concatenate(columns, axis=0)
    pieces = [column, matched(column, 0), matched(column, 1)]
    pieces += [flipped(piece, 1) for piece in pieces]
    return tiles(tile_list[0], tile_count, pair_mask[0], pieces)[None]


def solution(mesh):
    def run(*arrays):
        with jax.sharding.use_abstract_mesh(mesh.abstract_mesh):
            return jax.shard_map(
                body,
                mesh=mesh,
                in_specs=(
                    P("band", "dev", None),
                    P("band", "dev", None),
                    P("band", "dev"),
                    P("band", "dev", None),
                ),
                out_specs=P("band", "dev", None),
                check_vma=False,
            )(*arrays)

    return run
```

```python
import functools

import jax
import jax.numpy as jnp
from jax import lax
from jax.experimental import pallas as pl
from jax.experimental.pallas import tpu as pltpu
from jax.sharding import PartitionSpec as P

TILE = 64
LANES = 128
SHIFTS = 32
DEPTH = 3
SLOTS = 4
ALT_ROWS = 16
PREPARE_AT = 4
STAGE_AT = 20


def normalized(rows):
    values = rows.astype(jnp.float32)
    energy = jnp.sum(values * values, axis=-1, keepdims=True) + 1e-06
    return (values / jnp.sqrt(energy)).astype(jnp.bfloat16).astype(jnp.float32)


def select_block(refs, place, picks):
    block = refs[-1][place]
    for ref, pick in zip(refs[:-1], picks[:-1]):
        block = lax.select(pick, ref[place], block)
    return block


def tiles_kernel(list_ref, count_ref, mask_ref, *refs):
    pieces, (out_ref, units, later, alts, columns, peaks) = refs[:6], refs[6:]
    slots = out_ref.shape[0]
    samples = units.shape[1]
    used = count_ref[0, 0]
    band = lax.axis_index("band")
    dev = lax.axis_index("dev")
    lane = lax.broadcasted_iota(jnp.int32, (TILE, LANES), 1)
    wide = lax.broadcasted_iota(jnp.int32, (TILE, samples), 1)
    sign = jnp.where(wide % 2 == 0, 1.0, -1.0)

    def place_of(block):
        return (block // 2) ^ (dev // 2), (block + dev) % 2 == 0

    def run(acc_alt, *accs):
        acc_cyc, acc_neg = accs[: len(accs) // 2], accs[len(accs) // 2 :]
        count = len(acc_cyc) // 2

        def prepare(slot):
            place, same = place_of(list_ref[slot, 0])
            unit = normalized(select_block([pieces[0], pieces[3]], place, [same, None]))
            later[...] = unit
            alt = jnp.sum(unit * sign, axis=-1, keepdims=True) * (1.0 / samples)
            alts[...] = jnp.broadcast_to(alt, (TILE, LANES))
            offset = list_ref[slot, 1]
            place, same = place_of(list_ref[slot, 2])
            first = (band + offset // 2) % 2 == 1
            kinds = [offset == 1, (offset != 1) & first, (offset != 1) & jnp.logical_not(first)]
            picks = [kind & same for kind in kinds] + [kind & jnp.logical_not(same) for kind in kinds]
            half = normalized(select_block(pieces, place, picks)) * 0.5
            cyc, neg = [], []
            for r in range(samples // TILE):
                shifted = pltpu.roll(half, SHIFTS * r, 1) if r else half
                cyc.append(shifted.astype(jnp.bfloat16))
                neg.append(jnp.where(wide < SHIFTS * r, -shifted, shifted).astype(jnp.bfloat16))
            columns[0] = jnp.concatenate(cyc, axis=0)
            columns[1] = jnp.concatenate(neg, axis=0)

        def stage():
            for unit in range(2):
                pltpu.matmul_push_rhs(columns[unit], 0, unit, transpose=True)

        def push(s):
            at = 2 * (s % count)
            low, high = units[:, :LANES], units[:, LANES:]
            first = pltpu.roll(low, LANES - s, 1) if s else low
            second = pltpu.roll(high, LANES - s, 1) if s else high
            inside = lane < LANES - s
            a = jnp.where(inside, first, second).astype(jnp.bfloat16)
            b = jnp.where(inside, second, first).astype(jnp.bfloat16)
            c = jnp.where(inside, second, -first).astype(jnp.bfloat16)
            new = 0 if s == 0 else None
            pltpu.matmul_acc_lhs(acc_cyc[at], jnp.concatenate([a, b], axis=1), load_staged_rhs=new)
            pltpu.matmul_acc_lhs(acc_neg[at], jnp.concatenate([a, c], axis=1), load_staged_rhs=new)
            if s == 0:
                pltpu.matmul_acc_lhs(acc_alt, sign[:ALT_ROWS].astype(jnp.bfloat16))
            pltpu.matmul_acc_lhs(acc_cyc[at + 1], jnp.concatenate([b, a], axis=1))
            pltpu.matmul_acc_lhs(acc_neg[at + 1], jnp.concatenate([c, -a], axis=1))

        def one_slot(slot, more):
            best = [jnp.full((TILE, samples), -jnp.inf, jnp.float32)] * 2
            for s in range(SHIFTS):
                if s + DEPTH < SHIFTS:
                    push(s + DEPTH)
                elif more:
                    if s + DEPTH == SHIFTS:
                        units[...] = later[...]
                    push(s + DEPTH - SHIFTS)
                if s == 0:
                    nyquist = alts[:, :1] * pltpu.matmul_pop(acc_alt)[0:1]
                at = 2 * (s % count)
                for t in range(2):
                    pair = pltpu.matmul_pop(acc_cyc[at + t]) + jnp.abs(
                        pltpu.matmul_pop(acc_neg[at + t])
                    )
                    best[s % 2] = jnp.maximum(best[s % 2], pair)
                if s == PREPARE_AT and more:
                    prepare(slot + 1)
                if s == STAGE_AT and more:
                    stage()
            peak = jnp.maximum(best[0] - nyquist, best[1] + nyquist)
            peak = jnp.maximum(peak[:, :LANES], peak[:, LANES:])
            peak = jnp.maximum(peak, pltpu.roll(peak, TILE, 1))
            peaks[pl.ds(pl.multiple_of(slot * TILE, TILE), TILE), :] = peak

        prepare(0)
        stage()
        units[...] = later[...]
        for s in range(DEPTH):
            push(s)
        peaks[...] = jnp.zeros_like(peaks)

        def next_slot(slot, carry):
            one_slot(slot, True)
            return carry

        lax.fori_loop(0, used - 1, next_slot, 0)
        one_slot(used - 1, False)

    pl.run_scoped(
        run,
        pltpu.ACC(0)((ALT_ROWS, samples), jnp.float32),
        *[pltpu.ACC(unit)((TILE, samples), jnp.float32) for unit in range(2) for _ in range(2 * SLOTS)],
    )
    lane = lax.broadcasted_iota(jnp.int32, (slots, LANES), 1)
    for p in range(TILE // 2):
        even = peaks[pl.ds(2 * p, slots, stride=TILE), :]
        odd = peaks[pl.ds(2 * p + 1, slots, stride=TILE), :]
        at = pl.ds(p * LANES, LANES)
        out_ref[:, at] = jnp.where(lane < TILE, even, odd) * mask_ref[:, at].astype(jnp.float32)


def tiles(tile_list, tile_count, pair_mask, pieces):
    slots = tile_list.shape[0]
    samples = pieces[0].shape[2]
    smem = pl.BlockSpec(memory_space=pltpu.SMEM)
    vmem = pl.BlockSpec(memory_space=pltpu.VMEM)
    return pl.pallas_call(
        tiles_kernel,
        out_shape=jax.ShapeDtypeStruct(pair_mask.shape, jnp.float32),
        in_specs=[smem, smem, vmem] + [vmem] * 6,
        out_specs=vmem,
        scratch_shapes=[
            pltpu.VMEM((TILE, samples), jnp.float32),
            pltpu.VMEM((TILE, samples), jnp.float32),
            pltpu.VMEM((TILE, LANES), jnp.float32),
            pltpu.VMEM((2, samples, samples), jnp.bfloat16),
            pltpu.VMEM((slots * TILE, LANES), jnp.float32),
        ],
        compiler_params=pltpu.CompilerParams(vmem_limit_bytes=16 * 1024 * 1024),
        name="tiles",
    )(tile_list, tile_count, pair_mask, *pieces)


def matched(value, first):
    count = lax.axis_size("band")
    pairs = []
    for i in range(first, count - 1, 2):
        pairs += [(i, i + 1), (i + 1, i)]
    return lax.ppermute(value, "band", pairs)


def flipped(value, mask):
    return lax.ppermute(value, "dev", [(i, i ^ mask) for i in range(lax.axis_size("dev"))])


def body(waves, tile_list, tile_count, pair_mask):
    columns = [waves] + [flipped(waves, 2 * k) for k in range(1, lax.axis_size("dev") // 2)]
    column = jnp.concatenate(columns, axis=0)
    pieces = [column, matched(column, 0), matched(column, 1)]
    pieces += [flipped(piece, 1) for piece in pieces]
    return tiles(tile_list[0], tile_count, pair_mask[0], pieces)[None]


def solution(mesh):
    def run(*arrays):
        with jax.sharding.use_abstract_mesh(mesh.abstract_mesh):
            return jax.shard_map(
                body,
                mesh=mesh,
                in_specs=(
                    P("band", "dev", None),
                    P("band", "dev", None),
                    P("band", "dev"),
                    P("band", "dev", None),
                ),
                out_specs=P("band", "dev", None),
                check_vma=False,
            )(*arrays)

    return run
```

```python
import functools

import jax
import jax.numpy as jnp
from jax import lax
from jax.experimental import pallas as pl
from jax.experimental.pallas import tpu as pltpu
from jax.sharding import PartitionSpec as P

TILE = 64
LANES = 128
SHIFTS = 32
DEPTH = 3
SLOTS = 4
ALT_ROWS = 16
PREPARE_AT = 4
STAGE_AT = 20


def normalized(rows):
    values = rows.astype(jnp.float32)
    energy = jnp.sum(values * values, axis=-1, keepdims=True) + 1e-06
    return (values / jnp.sqrt(energy)).astype(jnp.bfloat16).astype(jnp.float32)


def tiles_kernel(list_ref, count_ref, mask_ref, *refs):
    same_ref, swapped_ref, out_ref, units, later, alts, columns, peaks = refs
    slots = out_ref.shape[0]
    samples = units.shape[1]
    used = count_ref[0, 0]
    band = lax.axis_index("band")
    dev = lax.axis_index("dev")
    lane = lax.broadcasted_iota(jnp.int32, (TILE, LANES), 1)
    wide = lax.broadcasted_iota(jnp.int32, (TILE, samples), 1)
    sign = jnp.where(wide % 2 == 0, 1.0, -1.0)

    columns_all = lax.axis_size("dev") // 2

    def block_at(block, offset):
        far = (block // 2) ^ (dev // 2)
        near = far < columns_all - 1
        place = far
        flips = band_flips()
        for k, flip in enumerate(flips):
            at = columns_all + jnp.where(
                near, k * (columns_all - 1) + far, len(flips) * (columns_all - 1) + k
            )
            place = jnp.where((band ^ flip) == band + offset - 1, at, place)
        return lax.select((block + dev) % 2 == 0, same_ref[place], swapped_ref[place])

    def run(acc_alt, *accs):
        acc_cyc, acc_neg = accs[: len(accs) // 2], accs[len(accs) // 2 :]
        count = len(acc_cyc) // 2

        def prepare(slot):
            unit = normalized(block_at(list_ref[slot, 0], jnp.int32(1)))
            later[...] = unit
            alt = jnp.sum(unit * sign, axis=-1, keepdims=True) * (1.0 / samples)
            alts[...] = jnp.broadcast_to(alt, (TILE, LANES))
            half = normalized(block_at(list_ref[slot, 2], list_ref[slot, 1])) * 0.5
            cyc, neg = [], []
            for r in range(samples // TILE):
                shifted = pltpu.roll(half, SHIFTS * r, 1) if r else half
                cyc.append(shifted.astype(jnp.bfloat16))
                neg.append(jnp.where(wide < SHIFTS * r, -shifted, shifted).astype(jnp.bfloat16))
            columns[0] = jnp.concatenate(cyc, axis=0)
            columns[1] = jnp.concatenate(neg, axis=0)

        def stage():
            for unit in range(2):
                pltpu.matmul_push_rhs(columns[unit], 0, unit, transpose=True)

        def push(s):
            at = 2 * (s % count)
            low, high = units[:, :LANES], units[:, LANES:]
            first = pltpu.roll(low, LANES - s, 1) if s else low
            second = pltpu.roll(high, LANES - s, 1) if s else high
            inside = lane < LANES - s
            a = jnp.where(inside, first, second).astype(jnp.bfloat16)
            b = jnp.where(inside, second, first).astype(jnp.bfloat16)
            c = jnp.where(inside, second, -first).astype(jnp.bfloat16)
            new = 0 if s == 0 else None
            pltpu.matmul_acc_lhs(acc_cyc[at], jnp.concatenate([a, b], axis=1), load_staged_rhs=new)
            pltpu.matmul_acc_lhs(acc_neg[at], jnp.concatenate([a, c], axis=1), load_staged_rhs=new)
            if s == 0:
                pltpu.matmul_acc_lhs(acc_alt, sign[:ALT_ROWS].astype(jnp.bfloat16))
            pltpu.matmul_acc_lhs(acc_cyc[at + 1], jnp.concatenate([b, a], axis=1))
            pltpu.matmul_acc_lhs(acc_neg[at + 1], jnp.concatenate([c, -a], axis=1))

        def one_slot(slot, more):
            best = [jnp.full((TILE, samples), -jnp.inf, jnp.float32)] * 2
            for s in range(SHIFTS):
                if s + DEPTH < SHIFTS:
                    push(s + DEPTH)
                elif more:
                    if s + DEPTH == SHIFTS:
                        units[...] = later[...]
                    push(s + DEPTH - SHIFTS)
                if s == 0:
                    nyquist = alts[:, :1] * pltpu.matmul_pop(acc_alt)[0:1]
                at = 2 * (s % count)
                for t in range(2):
                    pair = pltpu.matmul_pop(acc_cyc[at + t]) + jnp.abs(
                        pltpu.matmul_pop(acc_neg[at + t])
                    )
                    best[s % 2] = jnp.maximum(best[s % 2], pair)
                if s == PREPARE_AT and more:
                    prepare(slot + 1)
                if s == STAGE_AT and more:
                    stage()
            peak = jnp.maximum(best[0] - nyquist, best[1] + nyquist)
            peak = jnp.maximum(peak[:, :LANES], peak[:, LANES:])
            peak = jnp.maximum(peak, pltpu.roll(peak, TILE, 1))
            peaks[pl.ds(pl.multiple_of(slot * TILE, TILE), TILE), :] = peak

        prepare(0)
        stage()
        units[...] = later[...]
        for s in range(DEPTH):
            push(s)
        peaks[...] = jnp.zeros_like(peaks)

        def next_slot(slot, carry):
            one_slot(slot, True)
            return carry

        lax.fori_loop(0, used - 1, next_slot, 0)
        one_slot(used - 1, False)

    pl.run_scoped(
        run,
        pltpu.ACC(0)((ALT_ROWS, samples), jnp.float32),
        *[pltpu.ACC(unit)((TILE, samples), jnp.float32) for unit in range(2) for _ in range(2 * SLOTS)],
    )
    lane = lax.broadcasted_iota(jnp.int32, (slots, LANES), 1)
    for p in range(TILE // 2):
        even = peaks[pl.ds(2 * p, slots, stride=TILE), :]
        odd = peaks[pl.ds(2 * p + 1, slots, stride=TILE), :]
        at = pl.ds(p * LANES, LANES)
        out_ref[:, at] = jnp.where(lane < TILE, even, odd) * mask_ref[:, at].astype(jnp.float32)


def tiles(tile_list, tile_count, pair_mask, pieces):
    slots = tile_list.shape[0]
    samples = pieces[0].shape[2]
    smem = pl.BlockSpec(memory_space=pltpu.SMEM)
    vmem = pl.BlockSpec(memory_space=pltpu.VMEM)
    return pl.pallas_call(
        tiles_kernel,
        out_shape=jax.ShapeDtypeStruct(pair_mask.shape, jnp.float32),
        in_specs=[smem, smem, vmem, vmem, vmem],
        out_specs=vmem,
        scratch_shapes=[
            pltpu.VMEM((TILE, samples), jnp.float32),
            pltpu.VMEM((TILE, samples), jnp.float32),
            pltpu.VMEM((TILE, LANES), jnp.float32),
            pltpu.VMEM((2, samples, samples), jnp.bfloat16),
            pltpu.VMEM((slots * TILE, LANES), jnp.float32),
        ],
        compiler_params=pltpu.CompilerParams(vmem_limit_bytes=16 * 1024 * 1024),
        name="tiles",
    )(tile_list, tile_count, pair_mask, *pieces)


def band_flips():
    flips = [1]
    while flips[-1] < lax.axis_size("band") - 1:
        flips.append(2 * flips[-1] + 1)
    return flips


def permuted(value, partner):
    bands, devs = lax.axis_size("band"), lax.axis_size("dev")
    pairs = []
    for band in range(bands):
        for dev in range(devs):
            to_band, to_dev = partner(band, dev)
            pairs.append((band * devs + dev, to_band * devs + to_dev))
    return lax.ppermute(value, ("band", "dev"), pairs)


def from_column(value, flip):
    return permuted(value, lambda band, dev: (band, dev ^ (2 * flip)))


def from_core(value):
    return permuted(value, lambda band, dev: (band, dev ^ 1))


def from_band(value, flip):
    def partner(band, dev):
        if abs((band ^ flip) - band) == 1:
            return band ^ flip, dev
        return band, dev ^ 1

    return permuted(value, partner)


def body(waves, tile_list, tile_count, pair_mask):
    columns = [waves] + [from_column(waves, k) for k in range(1, lax.axis_size("dev") // 2)]
    near = jnp.concatenate(columns[:-1], axis=0)
    far = columns[-1]
    flips = band_flips()
    parts = [near, far]
    parts += [from_band(near, flip) for flip in flips]
    parts += [from_band(far, flip) for flip in flips]
    same = jnp.concatenate(parts, axis=0)
    return tiles(tile_list[0], tile_count, pair_mask[0], [same, from_core(same)])[None]


def solution(mesh):
    def run(*arrays):
        with jax.sharding.use_abstract_mesh(mesh.abstract_mesh):
            return jax.shard_map(
                body,
                mesh=mesh,
                in_specs=(
                    P("band", "dev", None),
                    P("band", "dev", None),
                    P("band", "dev"),
                    P("band", "dev", None),
                ),
                out_specs=P("band", "dev", None),
                check_vma=False,
            )(*arrays)

    return run
```

```python
import functools

import jax
import jax.numpy as jnp
from jax import lax
from jax.experimental import pallas as pl
from jax.experimental.pallas import tpu as pltpu
from jax.sharding import PartitionSpec as P

TILE = 64
LANES = 128
SHIFTS = 32
DEPTH = 3
SLOTS = 4
ALT_ROWS = 16
PREPARE_AT = 4
STAGE_AT = 20


def normalized(rows):
    values = rows.astype(jnp.float32)
    energy = jnp.sum(values * values, axis=-1, keepdims=True) + 1e-06
    return (values / jnp.sqrt(energy)).astype(jnp.bfloat16).astype(jnp.float32)


def tiles_kernel(list_ref, count_ref, mask_ref, *refs):
    same_ref, swapped_ref, out_ref, units, later, alts, columns, peaks = refs
    slots = out_ref.shape[0]
    samples = units.shape[1]
    used = count_ref[0, 0]
    band = lax.axis_index("band")
    dev = lax.axis_index("dev")
    lane = lax.broadcasted_iota(jnp.int32, (TILE, LANES), 1)
    wide = lax.broadcasted_iota(jnp.int32, (TILE, samples), 1)
    sign = jnp.where(wide % 2 == 0, 1.0, -1.0)

    columns_all = lax.axis_size("dev") // 2

    entries = list_ref[...]
    slot_at = lax.broadcasted_iota(jnp.int32, entries.shape, 2)

    def entry(column, slot):
        return jnp.sum(jnp.where(slot_at == slot, entries, 0)[column])

    def block_at(block, offset):
        far = (block // 2) ^ (dev // 2)
        near = far < columns_all - 1
        place = far
        flips = band_flips()
        for k, flip in enumerate(flips):
            at = columns_all + jnp.where(
                near, k * (columns_all - 1) + far, len(flips) * (columns_all - 1) + k
            )
            place = jnp.where((band ^ flip) == band + offset - 1, at, place)
        return lax.select((block + dev) % 2 == 0, same_ref[place], swapped_ref[place])

    def run(acc_alt, *accs):
        acc_cyc, acc_neg = accs[: len(accs) // 2], accs[len(accs) // 2 :]
        count = len(acc_cyc) // 2

        def prepare(slot):
            unit = normalized(block_at(entry(0, slot), jnp.int32(1)))
            later[...] = unit
            alt = jnp.sum(unit * sign, axis=-1, keepdims=True) * (1.0 / samples)
            alts[...] = jnp.broadcast_to(alt, (TILE, LANES))
            half = normalized(block_at(entry(2, slot), entry(1, slot))) * 0.5
            cyc, neg = [], []
            for r in range(samples // TILE):
                shifted = pltpu.roll(half, SHIFTS * r, 1) if r else half
                cyc.append(shifted.astype(jnp.bfloat16))
                neg.append(jnp.where(wide < SHIFTS * r, -shifted, shifted).astype(jnp.bfloat16))
            columns[0] = jnp.concatenate(cyc, axis=0)
            columns[1] = jnp.concatenate(neg, axis=0)

        def stage():
            for unit in range(2):
                pltpu.matmul_push_rhs(columns[unit], 0, unit, transpose=True)

        def push(s):
            at = 2 * (s % count)
            low, high = units[:, :LANES], units[:, LANES:]
            first = pltpu.roll(low, LANES - s, 1) if s else low
            second = pltpu.roll(high, LANES - s, 1) if s else high
            inside = lane < LANES - s
            a = jnp.where(inside, first, second).astype(jnp.bfloat16)
            b = jnp.where(inside, second, first).astype(jnp.bfloat16)
            c = jnp.where(inside, second, -first).astype(jnp.bfloat16)
            new = 0 if s == 0 else None
            pltpu.matmul_acc_lhs(acc_cyc[at], jnp.concatenate([a, b], axis=1), load_staged_rhs=new)
            pltpu.matmul_acc_lhs(acc_neg[at], jnp.concatenate([a, c], axis=1), load_staged_rhs=new)
            if s == 0:
                pltpu.matmul_acc_lhs(acc_alt, sign[:ALT_ROWS].astype(jnp.bfloat16))
            pltpu.matmul_acc_lhs(acc_cyc[at + 1], jnp.concatenate([b, a], axis=1))
            pltpu.matmul_acc_lhs(acc_neg[at + 1], jnp.concatenate([c, -a], axis=1))

        def one_slot(slot, more):
            best = [jnp.full((TILE, samples), -jnp.inf, jnp.float32)] * 2
            for s in range(SHIFTS):
                if s + DEPTH < SHIFTS:
                    push(s + DEPTH)
                elif more:
                    if s + DEPTH == SHIFTS:
                        units[...] = later[...]
                    push(s + DEPTH - SHIFTS)
                if s == 0:
                    nyquist = alts[:, :1] * pltpu.matmul_pop(acc_alt)[0:1]
                at = 2 * (s % count)
                for t in range(2):
                    pair = pltpu.matmul_pop(acc_cyc[at + t]) + jnp.abs(
                        pltpu.matmul_pop(acc_neg[at + t])
                    )
                    best[s % 2] = jnp.maximum(best[s % 2], pair)
                if s == PREPARE_AT and more:
                    prepare(slot + 1)
                if s == STAGE_AT and more:
                    stage()
            peak = jnp.maximum(best[0] - nyquist, best[1] + nyquist)
            peak = jnp.maximum(peak[:, :LANES], peak[:, LANES:])
            peak = jnp.maximum(peak, pltpu.roll(peak, TILE, 1))
            peaks[pl.ds(pl.multiple_of(slot * TILE, TILE), TILE), :] = peak

        prepare(0)
        stage()
        units[...] = later[...]
        for s in range(DEPTH):
            push(s)
        peaks[...] = jnp.zeros_like(peaks)

        def next_slot(slot, carry):
            one_slot(slot, True)
            return carry

        @pl.when(used == slots)
        def _():
            for slot in range(slots):
                one_slot(slot, slot < slots - 1)

        @pl.when(used < slots)
        def _():
            lax.fori_loop(0, used - 1, next_slot, 0)
            one_slot(used - 1, False)

    pl.run_scoped(
        run,
        pltpu.ACC(0)((ALT_ROWS, samples), jnp.float32),
        *[pltpu.ACC(unit)((TILE, samples), jnp.float32) for unit in range(2) for _ in range(2 * SLOTS)],
    )
    lane = lax.broadcasted_iota(jnp.int32, (slots, LANES), 1)
    for p in range(TILE // 2):
        even = peaks[pl.ds(2 * p, slots, stride=TILE), :]
        odd = peaks[pl.ds(2 * p + 1, slots, stride=TILE), :]
        at = pl.ds(p * LANES, LANES)
        out_ref[:, at] = jnp.where(lane < TILE, even, odd) * mask_ref[:, at].astype(jnp.float32)


def tiles(tile_list, tile_count, pair_mask, pieces):
    slots = pair_mask.shape[0]
    samples = pieces[0].shape[2]
    smem = pl.BlockSpec(memory_space=pltpu.SMEM)
    vmem = pl.BlockSpec(memory_space=pltpu.VMEM)
    return pl.pallas_call(
        tiles_kernel,
        out_shape=jax.ShapeDtypeStruct(pair_mask.shape, jnp.float32),
        in_specs=[vmem, smem, vmem, vmem, vmem],
        out_specs=vmem,
        scratch_shapes=[
            pltpu.VMEM((TILE, samples), jnp.float32),
            pltpu.VMEM((TILE, samples), jnp.float32),
            pltpu.VMEM((TILE, LANES), jnp.float32),
            pltpu.VMEM((2, samples, samples), jnp.bfloat16),
            pltpu.VMEM((slots * TILE, LANES), jnp.float32),
        ],
        compiler_params=pltpu.CompilerParams(vmem_limit_bytes=16 * 1024 * 1024),
        name="tiles",
    )(tile_list, tile_count, pair_mask, *pieces)


def band_flips():
    flips = [1]
    while flips[-1] < lax.axis_size("band") - 1:
        flips.append(2 * flips[-1] + 1)
    return flips


def permuted(value, partner):
    bands, devs = lax.axis_size("band"), lax.axis_size("dev")
    pairs = []
    for band in range(bands):
        for dev in range(devs):
            to_band, to_dev = partner(band, dev)
            pairs.append((band * devs + dev, to_band * devs + to_dev))
    return lax.ppermute(value, ("band", "dev"), pairs)


def from_column(value, flip):
    return permuted(value, lambda band, dev: (band, dev ^ (2 * flip)))


def from_core(value):
    return permuted(value, lambda band, dev: (band, dev ^ 1))


def from_band(value, flip):
    def partner(band, dev):
        if abs((band ^ flip) - band) == 1:
            return band ^ flip, dev
        return band, dev ^ 1

    return permuted(value, partner)


def body(waves, tile_list, tile_count, pair_mask):
    columns = [waves] + [from_column(waves, k) for k in range(1, lax.axis_size("dev") // 2)]
    near = jnp.concatenate(columns[:-1], axis=0)
    far = columns[-1]
    flips = band_flips()
    parts = [near, far]
    parts += [from_band(near, flip) for flip in flips]
    parts += [from_band(far, flip) for flip in flips]
    same = jnp.concatenate(parts, axis=0)
    return tiles(tile_list.transpose(2, 0, 1), tile_count, pair_mask[0], [same, from_core(same)])[None]


def solution(mesh):
    def run(*arrays):
        with jax.sharding.use_abstract_mesh(mesh.abstract_mesh):
            return jax.shard_map(
                body,
                mesh=mesh,
                in_specs=(
                    P("band", "dev", None),
                    P("band", "dev", None),
                    P("band", "dev"),
                    P("band", "dev", None),
                ),
                out_specs=P("band", "dev", None),
                check_vma=False,
            )(*arrays)

    return run
```

```python
import functools

import jax
import jax.numpy as jnp
from jax import lax
from jax.experimental import pallas as pl
from jax.experimental.pallas import tpu as pltpu
from jax.sharding import PartitionSpec as P

TILE = 64
LANES = 128
SHIFTS = 32
DEPTH = 3
SLOTS = 4
ALT_ROWS = 16
PREPARE_AT = 4
STAGE_AT = 20


def normalized(rows):
    values = rows.astype(jnp.float32)
    energy = jnp.sum(values * values, axis=-1, keepdims=True) + 1e-06
    return (values / jnp.sqrt(energy)).astype(jnp.bfloat16).astype(jnp.float32)


def tiles_kernel(list_ref, count_ref, mask_ref, *refs):
    same_ref, swapped_ref, out_ref, units, later, alts, columns, peaks = refs
    slots = out_ref.shape[0]
    samples = units.shape[1]
    used = count_ref[0, 0]
    band = lax.axis_index("band")
    dev = lax.axis_index("dev")
    lane = lax.broadcasted_iota(jnp.int32, (TILE, LANES), 1)
    wide = lax.broadcasted_iota(jnp.int32, (TILE, samples), 1)
    sign = jnp.where(wide % 2 == 0, 1.0, -1.0)

    columns_all = lax.axis_size("dev") // 2

    entries = list_ref[...]
    slot_at = lax.broadcasted_iota(jnp.int32, entries.shape, 2)

    def entry(column, slot):
        return jnp.sum(jnp.where(slot_at == slot, entries, 0)[column])

    def block_at(block, offset):
        column = (block // 2) ^ (dev // 2)
        near = column < columns_all - 1
        far = jnp.where((column > 0) & near, columns_all - 1 - column, column)
        place = far
        flips = band_flips()
        for k, flip in enumerate(flips):
            at = columns_all + jnp.where(
                near, k * (columns_all - 1) + far, len(flips) * (columns_all - 1) + k
            )
            place = jnp.where((band ^ flip) == band + offset - 1, at, place)
        return lax.select((block + dev) % 2 == 0, same_ref[place], swapped_ref[place])

    def run(acc_alt, *accs):
        acc_cyc, acc_neg = accs[: len(accs) // 2], accs[len(accs) // 2 :]
        count = len(acc_cyc) // 2

        def prepare(slot):
            unit = normalized(block_at(entry(0, slot), jnp.int32(1)))
            later[...] = unit
            alt = jnp.sum(unit * sign, axis=-1, keepdims=True) * (1.0 / samples)
            alts[...] = jnp.broadcast_to(alt, (TILE, LANES))
            half = normalized(block_at(entry(2, slot), entry(1, slot))) * 0.5
            cyc, neg = [], []
            for r in range(samples // TILE):
                shifted = pltpu.roll(half, SHIFTS * r, 1) if r else half
                cyc.append(shifted.astype(jnp.bfloat16))
                neg.append(jnp.where(wide < SHIFTS * r, -shifted, shifted).astype(jnp.bfloat16))
            columns[0] = jnp.concatenate(cyc, axis=0)
            columns[1] = jnp.concatenate(neg, axis=0)

        def stage():
            for unit in range(2):
                pltpu.matmul_push_rhs(columns[unit], 0, unit, transpose=True)

        def push(s):
            at = 2 * (s % count)
            low, high = units[:, :LANES], units[:, LANES:]
            first = pltpu.roll(low, LANES - s, 1) if s else low
            second = pltpu.roll(high, LANES - s, 1) if s else high
            inside = lane < LANES - s
            a = jnp.where(inside, first, second).astype(jnp.bfloat16)
            b = jnp.where(inside, second, first).astype(jnp.bfloat16)
            c = jnp.where(inside, second, -first).astype(jnp.bfloat16)
            new = 0 if s == 0 else None
            pltpu.matmul_acc_lhs(acc_cyc[at], jnp.concatenate([a, b], axis=1), load_staged_rhs=new)
            pltpu.matmul_acc_lhs(acc_neg[at], jnp.concatenate([a, c], axis=1), load_staged_rhs=new)
            if s == 0:
                pltpu.matmul_acc_lhs(acc_alt, sign[:ALT_ROWS].astype(jnp.bfloat16))
            pltpu.matmul_acc_lhs(acc_cyc[at + 1], jnp.concatenate([b, a], axis=1))
            pltpu.matmul_acc_lhs(acc_neg[at + 1], jnp.concatenate([c, -a], axis=1))

        def one_slot(slot, more):
            best = [jnp.full((TILE, samples), -jnp.inf, jnp.float32)] * 2
            for s in range(SHIFTS):
                if s + DEPTH < SHIFTS:
                    push(s + DEPTH)
                elif more:
                    if s + DEPTH == SHIFTS:
                        units[...] = later[...]
                    push(s + DEPTH - SHIFTS)
                if s == 0:
                    nyquist = alts[:, :1] * pltpu.matmul_pop(acc_alt)[0:1]
                at = 2 * (s % count)
                for t in range(2):
                    pair = pltpu.matmul_pop(acc_cyc[at + t]) + jnp.abs(
                        pltpu.matmul_pop(acc_neg[at + t])
                    )
                    best[s % 2] = jnp.maximum(best[s % 2], pair)
                if s == PREPARE_AT and more:
                    prepare(slot + 1)
                if s == STAGE_AT and more:
                    stage()
            peak = jnp.maximum(best[0] - nyquist, best[1] + nyquist)
            peak = jnp.maximum(peak[:, :LANES], peak[:, LANES:])
            peak = jnp.maximum(peak, pltpu.roll(peak, TILE, 1))
            peaks[pl.ds(pl.multiple_of(slot * TILE, TILE), TILE), :] = peak

        prepare(0)
        stage()
        units[...] = later[...]
        for s in range(DEPTH):
            push(s)
        peaks[...] = jnp.zeros_like(peaks)

        def next_slot(slot, carry):
            one_slot(slot, True)
            return carry

        @pl.when(used == slots)
        def _():
            for slot in range(slots):
                one_slot(slot, slot < slots - 1)

        @pl.when(used < slots)
        def _():
            lax.fori_loop(0, used - 1, next_slot, 0)
            one_slot(used - 1, False)

    pl.run_scoped(
        run,
        pltpu.ACC(0)((ALT_ROWS, samples), jnp.float32),
        *[pltpu.ACC(unit)((TILE, samples), jnp.float32) for unit in range(2) for _ in range(2 * SLOTS)],
    )
    lane = lax.broadcasted_iota(jnp.int32, (slots, LANES), 1)
    for p in range(TILE // 2):
        even = peaks[pl.ds(2 * p, slots, stride=TILE), :]
        odd = peaks[pl.ds(2 * p + 1, slots, stride=TILE), :]
        at = pl.ds(p * LANES, LANES)
        out_ref[:, at] = jnp.where(lane < TILE, even, odd) * mask_ref[:, at].astype(jnp.float32)


def tiles(tile_list, tile_count, pair_mask, pieces):
    slots = pair_mask.shape[0]
    samples = pieces[0].shape[2]
    smem = pl.BlockSpec(memory_space=pltpu.SMEM)
    vmem = pl.BlockSpec(memory_space=pltpu.VMEM)
    return pl.pallas_call(
        tiles_kernel,
        out_shape=jax.ShapeDtypeStruct(pair_mask.shape, jnp.float32),
        in_specs=[vmem, smem, vmem, vmem, vmem],
        out_specs=vmem,
        scratch_shapes=[
            pltpu.VMEM((TILE, samples), jnp.float32),
            pltpu.VMEM((TILE, samples), jnp.float32),
            pltpu.VMEM((TILE, LANES), jnp.float32),
            pltpu.VMEM((2, samples, samples), jnp.bfloat16),
            pltpu.VMEM((slots * TILE, LANES), jnp.float32),
        ],
        compiler_params=pltpu.CompilerParams(vmem_limit_bytes=16 * 1024 * 1024),
        name="tiles",
    )(tile_list, tile_count, pair_mask, *pieces)


def band_flips():
    flips = [1]
    while flips[-1] < lax.axis_size("band") - 1:
        flips.append(2 * flips[-1] + 1)
    return flips


def permuted(value, partner):
    bands, devs = lax.axis_size("band"), lax.axis_size("dev")
    pairs = []
    for band in range(bands):
        for dev in range(devs):
            to_band, to_dev = partner(band, dev)
            pairs.append((band * devs + dev, to_band * devs + to_dev))
    return lax.ppermute(value, ("band", "dev"), pairs)


def from_column(value, flip):
    return permuted(value, lambda band, dev: (band, dev ^ (2 * flip)))


def from_core(value):
    return permuted(value, lambda band, dev: (band, dev ^ 1))


def from_band(value, flip):
    def partner(band, dev):
        if abs((band ^ flip) - band) == 1:
            return band ^ flip, dev
        return band, dev ^ 1

    return permuted(value, partner)


def body(waves, tile_list, tile_count, pair_mask):
    columns = [waves] + [from_column(waves, k) for k in range(1, lax.axis_size("dev") // 2)]
    near = jnp.concatenate(columns[:1] + columns[-2:0:-1], axis=0)
    far = columns[-1]
    flips = band_flips()
    parts = [near, far]
    parts += [from_band(near, flip) for flip in flips]
    parts += [from_band(far, flip) for flip in flips]
    same = jnp.concatenate(parts, axis=0)
    return tiles(tile_list.transpose(2, 0, 1), tile_count, pair_mask[0], [same, from_core(same)])[None]


def solution(mesh):
    def run(*arrays):
        with jax.sharding.use_abstract_mesh(mesh.abstract_mesh):
            return jax.shard_map(
                body,
                mesh=mesh,
                in_specs=(
                    P("band", "dev", None),
                    P("band", "dev", None),
                    P("band", "dev"),
                    P("band", "dev", None),
                ),
                out_specs=P("band", "dev", None),
                check_vma=False,
            )(*arrays)

    return run
```

```python
import functools

import jax
import jax.numpy as jnp
from jax import lax
from jax.experimental import pallas as pl
from jax.experimental.pallas import tpu as pltpu
from jax.sharding import PartitionSpec as P

TILE = 64
LANES = 128
SHIFTS = 32
DEPTH = 3
SLOTS = 4
ALT_ROWS = 16
PREPARE_AT = 4
STAGE_AT = 20


def normalized(rows):
    values = rows.astype(jnp.float32)
    energy = jnp.sum(values * values, axis=-1, keepdims=True) + 1e-06
    return (values / jnp.sqrt(energy)).astype(jnp.bfloat16).astype(jnp.float32)


def tiles_kernel(list_ref, count_ref, mask_ref, *refs):
    same_ref, swapped_ref, out_ref, units, later, alts, columns, peaks = refs
    slots = out_ref.shape[0]
    samples = units.shape[1]
    used = count_ref[0, 0]
    band = lax.axis_index("band")
    dev = lax.axis_index("dev")
    lane = lax.broadcasted_iota(jnp.int32, (TILE, LANES), 1)
    wide = lax.broadcasted_iota(jnp.int32, (TILE, samples), 1)
    sign = jnp.where(wide % 2 == 0, 1.0, -1.0)

    columns_all = lax.axis_size("dev") // 2

    entries = list_ref[...]
    slot_at = lax.broadcasted_iota(jnp.int32, entries.shape, 2)

    def entry(column, slot):
        return jnp.sum(jnp.where(slot_at == slot, entries, 0)[column])

    def block_at(block, offset):
        column = (block // 2) ^ (dev // 2)
        place = column
        flips = band_flips()
        near = columns_all
        far = near + sum(split_at(k, columns_all) for k in range(len(flips)))
        for k, flip in enumerate(flips):
            split = split_at(k, columns_all)
            at = jnp.where(column < split, near + column, far + column - split)
            place = jnp.where((band ^ flip) == band + offset - 1, at, place)
            near, far = near + split, far + columns_all - split
        return lax.select((block + dev) % 2 == 0, same_ref[place], swapped_ref[place])

    def run(acc_alt, *accs):
        acc_cyc, acc_neg = accs[: len(accs) // 2], accs[len(accs) // 2 :]
        count = len(acc_cyc) // 2

        def prepare(slot):
            unit = normalized(block_at(entry(0, slot), jnp.int32(1)))
            later[...] = unit
            alt = jnp.sum(unit * sign, axis=-1, keepdims=True) * (1.0 / samples)
            alts[...] = jnp.broadcast_to(alt, (TILE, LANES))
            half = normalized(block_at(entry(2, slot), entry(1, slot))) * 0.5
            cyc, neg = [], []
            for r in range(samples // TILE):
                shifted = pltpu.roll(half, SHIFTS * r, 1) if r else half
                cyc.append(shifted.astype(jnp.bfloat16))
                neg.append(jnp.where(wide < SHIFTS * r, -shifted, shifted).astype(jnp.bfloat16))
            columns[0] = jnp.concatenate(cyc, axis=0)
            columns[1] = jnp.concatenate(neg, axis=0)

        def stage():
            for unit in range(2):
                pltpu.matmul_push_rhs(columns[unit], 0, unit, transpose=True)

        def push(s):
            at = 2 * (s % count)
            low, high = units[:, :LANES], units[:, LANES:]
            first = pltpu.roll(low, LANES - s, 1) if s else low
            second = pltpu.roll(high, LANES - s, 1) if s else high
            inside = lane < LANES - s
            a = jnp.where(inside, first, second).astype(jnp.bfloat16)
            b = jnp.where(inside, second, first).astype(jnp.bfloat16)
            c = jnp.where(inside, second, -first).astype(jnp.bfloat16)
            new = 0 if s == 0 else None
            pltpu.matmul_acc_lhs(acc_cyc[at], jnp.concatenate([a, b], axis=1), load_staged_rhs=new)
            pltpu.matmul_acc_lhs(acc_neg[at], jnp.concatenate([a, c], axis=1), load_staged_rhs=new)
            if s == 0:
                pltpu.matmul_acc_lhs(acc_alt, sign[:ALT_ROWS].astype(jnp.bfloat16))
            pltpu.matmul_acc_lhs(acc_cyc[at + 1], jnp.concatenate([b, a], axis=1))
            pltpu.matmul_acc_lhs(acc_neg[at + 1], jnp.concatenate([c, -a], axis=1))

        def one_slot(slot, more):
            best = [jnp.full((TILE, samples), -jnp.inf, jnp.float32)] * 2
            for s in range(SHIFTS):
                if s + DEPTH < SHIFTS:
                    push(s + DEPTH)
                elif more:
                    if s + DEPTH == SHIFTS:
                        units[...] = later[...]
                    push(s + DEPTH - SHIFTS)
                if s == 0:
                    nyquist = alts[:, :1] * pltpu.matmul_pop(acc_alt)[0:1]
                at = 2 * (s % count)
                for t in range(2):
                    pair = pltpu.matmul_pop(acc_cyc[at + t]) + jnp.abs(
                        pltpu.matmul_pop(acc_neg[at + t])
                    )
                    best[s % 2] = jnp.maximum(best[s % 2], pair)
                if s == PREPARE_AT and more:
                    prepare(slot + 1)
                if s == STAGE_AT and more:
                    stage()
            peak = jnp.maximum(best[0] - nyquist, best[1] + nyquist)
            peak = jnp.maximum(peak[:, :LANES], peak[:, LANES:])
            peak = jnp.maximum(peak, pltpu.roll(peak, TILE, 1))
            peaks[pl.ds(pl.multiple_of(slot * TILE, TILE), TILE), :] = peak

        prepare(0)
        stage()
        units[...] = later[...]
        for s in range(DEPTH):
            push(s)
        peaks[...] = jnp.zeros_like(peaks)

        def next_slot(slot, carry):
            one_slot(slot, True)
            return carry

        @pl.when(used == slots)
        def _():
            for slot in range(slots):
                one_slot(slot, slot < slots - 1)

        @pl.when(used < slots)
        def _():
            lax.fori_loop(0, used - 1, next_slot, 0)
            one_slot(used - 1, False)

    pl.run_scoped(
        run,
        pltpu.ACC(0)((ALT_ROWS, samples), jnp.float32),
        *[pltpu.ACC(unit)((TILE, samples), jnp.float32) for unit in range(2) for _ in range(2 * SLOTS)],
    )
    lane = lax.broadcasted_iota(jnp.int32, (slots, LANES), 1)
    for p in range(TILE // 2):
        even = peaks[pl.ds(2 * p, slots, stride=TILE), :]
        odd = peaks[pl.ds(2 * p + 1, slots, stride=TILE), :]
        at = pl.ds(p * LANES, LANES)
        out_ref[:, at] = jnp.where(lane < TILE, even, odd) * mask_ref[:, at].astype(jnp.float32)


def tiles(tile_list, tile_count, pair_mask, pieces):
    slots = pair_mask.shape[0]
    samples = pieces[0].shape[2]
    smem = pl.BlockSpec(memory_space=pltpu.SMEM)
    vmem = pl.BlockSpec(memory_space=pltpu.VMEM)
    return pl.pallas_call(
        tiles_kernel,
        out_shape=jax.ShapeDtypeStruct(pair_mask.shape, jnp.float32),
        in_specs=[vmem, smem, vmem, vmem, vmem],
        out_specs=vmem,
        scratch_shapes=[
            pltpu.VMEM((TILE, samples), jnp.float32),
            pltpu.VMEM((TILE, samples), jnp.float32),
            pltpu.VMEM((TILE, LANES), jnp.float32),
            pltpu.VMEM((2, samples, samples), jnp.bfloat16),
            pltpu.VMEM((slots * TILE, LANES), jnp.float32),
        ],
        compiler_params=pltpu.CompilerParams(vmem_limit_bytes=16 * 1024 * 1024),
        name="tiles",
    )(tile_list, tile_count, pair_mask, *pieces)


def band_flips():
    flips = [1]
    while flips[-1] < lax.axis_size("band") - 1:
        flips.append(2 * flips[-1] + 1)
    return flips


def split_at(k, columns):
    return columns - 1 if k else columns // 2


def permuted(value, partner):
    bands, devs = lax.axis_size("band"), lax.axis_size("dev")
    pairs = []
    for band in range(bands):
        for dev in range(devs):
            to_band, to_dev = partner(band, dev)
            pairs.append((band * devs + dev, to_band * devs + to_dev))
    return lax.ppermute(value, ("band", "dev"), pairs)


def from_column(value, flip):
    return permuted(value, lambda band, dev: (band, dev ^ (2 * flip)))


def from_core(value):
    return permuted(value, lambda band, dev: (band, dev ^ 1))


def from_band(value, flip):
    def partner(band, dev):
        if abs((band ^ flip) - band) == 1:
            return band ^ flip, dev
        return band, dev ^ 1

    return permuted(value, partner)


def body(waves, tile_list, tile_count, pair_mask):
    columns = [waves] + [from_column(waves, k) for k in range(1, lax.axis_size("dev") // 2)]
    parts = list(columns)
    for ahead in (True, False):
        for k, flip in enumerate(band_flips()):
            split = split_at(k, len(columns))
            blocks = columns[:split] if ahead else columns[split:]
            parts.append(from_band(jnp.concatenate(blocks, axis=0), flip))
    same = jnp.concatenate(parts, axis=0)
    return tiles(tile_list.transpose(2, 0, 1), tile_count, pair_mask[0], [same, from_core(same)])[None]


def solution(mesh):
    def run(*arrays):
        with jax.sharding.use_abstract_mesh(mesh.abstract_mesh):
            return jax.shard_map(
                body,
                mesh=mesh,
                in_specs=(
                    P("band", "dev", None),
                    P("band", "dev", None),
                    P("band", "dev"),
                    P("band", "dev", None),
                ),
                out_specs=P("band", "dev", None),
                check_vma=False,
            )(*arrays)

    return run
```
